32 devices in a mesh: groups: 2 (over x), ctx: 8 (over z, y), dp: 2 (over core).
Axes of the slice: x: 2, y: 2, z: 4, core: 2. Of those that a mesh axis runs over, the one named last changes fastest.
Arguments:
- tokens: bfloat16 [8, 1024, 4096], P(('groups', 'dp'), 'ctx'), parts along dimension 0, may hold values from -6 to 6
- norm_gain: float32 [4096], replicated, may hold values from 0.25 to 1.75
- w_query: bfloat16 [4096, 2048], P('dp')
- w_key: bfloat16 [4096, 2048], P('dp')
- w_value: bfloat16 [4096, 2048], P('dp'), may hold values from -0.09375 to 0.09375
- query_gain: float32 [2048], replicated
- key_gain: float32 [2048], replicated
- key_blocks: int32 [16, 5], P(('groups', 'ctx')), parts along dimension 0, may hold values from 0 to 7, as said below
Outputs:
- attended: bfloat16 [8, 1024, 2048], P(('groups', 'dp'), 'ctx'), parts along dimension 0
The draws below stay inside these ranges and needn't reach their ends.
There are 2 independent parts, one for each index of `groups`. The reference program is written for one: setup_inputs(seed, part) draws one part's arguments, and reference() takes and returns one part's arrays. A program takes and returns all parts, laid end to end along the dimension named above; an argument that names none is the same for every part. Nothing has to cross between parts.
Inputs may be any that keep to these rules, and one draw needn't show every extreme that they name: `key_blocks`: row b holds b - 1, b, b + 1 (modulo 8) and then two different blocks (b + 2 m) modulo 8 with m from 1 to 3.
All inputs are finite; a program needn't handle non-finite values.
Results may differ from the reference program's by a relative error of at most 0.012.
The reference program's roundings to bfloat16 on the way count: a program that leaves them out, or rounds other values in their place, can miss the bound.
Values may be sent and summed in bfloat16 or wider, within the bound.
A program may use at most 256 MiB of HBM per device.

```python
import jax
import jax.numpy as jnp
from jax import lax

D = 4096
HEADS = 16
HEAD_DIM = 128
BLOCK = 128
HH = 2048
BLOCKS = 8
SEQ_LEN = 1024
SEQS = 4


def query_key_pair(key):
    first = jax.random.normal(jax.random.fold_in(key, 11), (D, HH), jnp.float32) * D ** (-0.5)
    second = jax.random.normal(jax.random.fold_in(key, 12), (D, HH), jnp.float32) * D ** (-0.5)
    return (first, second)


def draw_w_query(key, part):
    return query_key_pair(key)[0].astype(jnp.bfloat16)


def draw_w_key(key, part):
    return query_key_pair(key)[1].astype(jnp.bfloat16)


def gain_pair(key):
    jitter_one = jax.random.uniform(jax.random.fold_in(key, 21), (HH,), jnp.float32, 0.7, 1.5)
    jitter_two = jax.random.uniform(jax.random.fold_in(key, 22), (HH,), jnp.float32, 0.7, 1.5)
    return (jitter_one, jitter_two)


def draw_query_gain(key, part):
    return gain_pair(key)[0]


def draw_key_gain(key, part):
    return gain_pair(key)[1]


def draw_key_blocks(key, part):
    half_loop = BLOCKS // 2
    block_ids = jnp.arange(BLOCKS, dtype=jnp.int32)
    popular = jax.random.randint(jax.random.fold_in(key, 31), (BLOCKS,), 0, 4)
    noise = jax.random.randint(jax.random.fold_in(key, 32), (BLOCKS, half_loop - 1), 0, 65536)
    targets = (block_ids[:, None] + 2 * jnp.arange(1, half_loop, dtype=jnp.int32)[None, :]) % BLOCKS
    ranking = (noise + jnp.take(popular, targets) * 65536) * half_loop + jnp.arange(half_loop - 1, dtype=jnp.int32)[None, :]
    picked = lax.top_k(ranking, 2)[1]
    distant = jnp.take_along_axis(targets, picked, axis=1)
    nearby = jnp.stack([(block_ids - 1) % BLOCKS, block_ids, (block_ids + 1) % BLOCKS], axis=1)
    return jnp.concatenate([nearby, distant], axis=1).astype(jnp.int32)


def block_scale(rng, extent, cuts, smallest, largest):
    loudness, own = 1.0, jax.random.fold_in(rng, 6)
    for dim, blocks in cuts:
        draws = jnp.exp(jax.random.uniform(jax.random.fold_in(own, dim), (blocks,), jnp.float32, smallest / len(cuts), largest / len(cuts)))
        loudness = loudness * jnp.repeat(draws, extent[dim] // blocks).reshape([-1 if axis == dim else 1 for axis in range(len(extent))])
    return loudness


def bell_draw(rng, shape, spread, limit, pieces=(), held_as=jnp.bfloat16):
    drawn = spread * jax.random.normal(rng, shape, jnp.float32)
    if pieces:
        drawn = drawn * block_scale(rng, shape, pieces, -0.22, 0.18)
    return jnp.clip(drawn, -limit, limit).astype(held_as)


def setup_inputs(seed: int = 0, part: int = 0) -> dict:
    key_of = jax.random.split(jax.random.key(seed), 9)
    part_keys = jax.random.split(jax.random.fold_in(key_of[8], part), 9)
    return {
        "tokens": bell_draw(part_keys[0], (SEQS, SEQ_LEN, D), 1.0, 6.0, ((0, 2), (1, 8))),
        "norm_gain": jnp.clip(1.0 + 0.15 * jax.random.normal(key_of[1], (D,), jnp.float32), 0.25, 1.75),
        "w_query": draw_w_query(jax.random.fold_in(key_of[8], 71), part),
        "w_key": draw_w_key(jax.random.fold_in(key_of[8], 71), part),
        "w_value": bell_draw(key_of[4], (D, HH), D ** -0.5, 0.09375, ((0, 2),)),
        "query_gain": draw_query_gain(jax.random.fold_in(key_of[8], 71), part),
        "key_gain": draw_key_gain(jax.random.fold_in(key_of[8], 71), part),
        "key_blocks": draw_key_blocks(jax.random.fold_in(jax.random.fold_in(key_of[8], part), 71), part),
    }


def head_norm(tensor, gain_row):
    shaped = tensor.reshape(SEQS, SEQ_LEN, HEADS, HEAD_DIM)
    mean_sq = lax.optimization_barrier(jnp.mean(shaped * shaped, axis=-1, keepdims=True))
    gains = gain_row.astype(jnp.float32).reshape(HEADS, HEAD_DIM)
    return (shaped * lax.rsqrt(mean_sq + 1e-06) * gains).astype(jnp.bfloat16)

def reference(tokens, norm_gain, w_query, w_key, w_value, query_gain, key_gain, key_blocks):
    wide = tokens.astype(jnp.float32)
    mean_sq = lax.optimization_barrier(jnp.mean(wide * wide, axis=-1, keepdims=True))
    normed = (wide * lax.rsqrt(mean_sq + 1e-06) * norm_gain.astype(jnp.float32)).astype(jnp.bfloat16)
    flat_rows = normed.reshape(SEQS * SEQ_LEN, D)
    query_raw = jnp.dot(flat_rows, w_query, preferred_element_type=jnp.float32)
    key_raw = jnp.dot(flat_rows, w_key, preferred_element_type=jnp.float32)
    value_raw = jnp.dot(flat_rows, w_value, preferred_element_type=jnp.float32)
    queries = head_norm(query_raw, query_gain)
    keys_all = head_norm(key_raw, key_gain)
    values_all = value_raw.astype(jnp.bfloat16).reshape(SEQS, SEQ_LEN, HEADS, HEAD_DIM)
    score_scale = 1.0 / float(HEAD_DIM) ** 0.5

    def one_block(inputs):
        block_index, listed = inputs
        query_rows = lax.dynamic_slice_in_dim(queries, (block_index * BLOCK).astype(jnp.int32), BLOCK, 1)
        row_index = (listed[:, None] * BLOCK + jnp.arange(BLOCK, dtype=jnp.int32)[None, :]).reshape(-1).astype(jnp.int32)
        key_rows = jnp.take(keys_all, row_index, axis=1)
        value_rows = jnp.take(values_all, row_index, axis=1)
        scores = jnp.einsum('sqhd,skhd->shqk', query_rows.astype(jnp.float32), key_rows.astype(jnp.float32)) * score_scale
        row_max = lax.optimization_barrier(jnp.max(scores, axis=-1, keepdims=True))
        expo = jnp.exp(scores - row_max)
        total = lax.optimization_barrier(jnp.sum(expo, axis=-1, keepdims=True))
        weights = expo.astype(jnp.bfloat16)
        mixed = jnp.einsum('shqk,skhd->sqhd', weights.astype(jnp.float32), value_rows.astype(jnp.float32))
        mixed = mixed / jnp.transpose(total, (0, 2, 1, 3))
        return mixed.astype(jnp.bfloat16).reshape(SEQS, BLOCK, HH)
    outputs = lax.map(one_block, (jnp.arange(BLOCKS, dtype=jnp.int32), key_blocks))
    return jnp.transpose(outputs, (1, 0, 2, 3)).reshape(SEQS, SEQ_LEN, HH)
```

```python
import functools

import jax
import jax.numpy as jnp
from jax import lax
from jax.experimental import pallas as pl
from jax.experimental.pallas import tpu as pltpu
from jax.sharding import PartitionSpec as P

HEAD_DIM = 128
EPS = 1e-06
LAG = 2
MESH = pl.DeviceIdType.MESH


def fused(
    n,
    tok_hbm, gain_ref, wq_hbm, wk_hbm, wv_hbm, qg_ref, kg_ref, kb_hbm,
    out_ref,
    tok, lhs, xsend, wbuf, pmine, psend, precv, send, recv_a, recv_b, obuf, kb_all, kb_smem,
    tok_sem, w_sem, x_ssem, x_rsem, p_ssem, p_rsem, a_ssem, a_rsem, o_ssem, o_rsem,
    kb_ssem, kb_rsem, kb_lsem,
):
    c = lax.axis_index("ctx")
    d = lax.axis_index("dp")
    seqs, rows, width = tok.shape
    half = width // 2
    cw = wbuf.shape[2] // 3
    heads = cw // HEAD_DIM
    recvs = (recv_a, recv_b)
    steps = seqs * n

    def peer(t):
        odd = t % 2
        off = n // 2 + (1 - odd) * (t // 2) - odd * ((t + 1) // 2)
        return (c + off) % n

    def tok_copy(s):
        return pltpu.make_async_copy(tok_hbm.at[s], tok.at[s], tok_sem.at[s])

    def w_copy(j, i):
        w = (wq_hbm, wk_hbm, wv_hbm)[i]
        return pltpu.make_async_copy(
            w.at[:, pl.ds(pl.multiple_of(j * cw, cw), cw)],
            wbuf.at[j, :, pl.ds(i * cw, cw)],
            w_sem.at[j, i],
        )

    def x_copy(s):
        return pltpu.make_async_remote_copy(
            src_ref=xsend.at[s], dst_ref=lhs.at[s, pl.ds(rows, rows)],
            send_sem=x_ssem.at[s], recv_sem=x_rsem.at[s],
            device_id={"dp": 1 - d}, device_id_type=MESH)

    def p_copy(u):
        return pltpu.make_async_remote_copy(
            src_ref=psend.at[u], dst_ref=precv.at[u],
            send_sem=p_ssem.at[u], recv_sem=p_rsem.at[u],
            device_id={"dp": 1 - d}, device_id_type=MESH)

    def a_copy(s, j, src):
        return pltpu.make_async_remote_copy(
            src_ref=send.at[s, j], dst_ref=recvs[s].at[src],
            send_sem=a_ssem.at[s, j], recv_sem=a_rsem.at[s, src],
            device_id={"ctx": j}, device_id_type=MESH)

    def o_copy(s, j, src):
        return pltpu.make_async_remote_copy(
            src_ref=obuf.at[s, j],
            dst_ref=out_ref.at[s, :, pl.ds(pl.multiple_of(src * cw, cw), cw)],
            send_sem=o_ssem.at[s, j], recv_sem=o_rsem.at[s, src],
            device_id={"ctx": j}, device_id_type=MESH)

    def kb_copy(j, src):
        return pltpu.make_async_remote_copy(
            src_ref=kb_hbm, dst_ref=kb_all.at[src],
            send_sem=kb_ssem.at[j], recv_sem=kb_rsem.at[src],
            device_id={"ctx": j}, device_id_type=MESH)

    for s in range(seqs):
        tok_copy(s).start()

    def start_weights(t, _):
        for i in range(3):
            w_copy(peer(t), i).start()
        return 0

    lax.fori_loop(0, n, start_weights, 0)

    barrier = pltpu.get_barrier_semaphore()
    pl.semaphore_signal(barrier, inc=1, device_id={"dp": 1 - d}, device_id_type=MESH)

    def greet(t, _):
        pl.semaphore_signal(barrier, inc=1, device_id={"ctx": peer(t)}, device_id_type=MESH)
        return 0

    lax.fori_loop(0, n - 1, greet, 0)

    mine = pl.ds(pl.multiple_of(d * half, half), half)
    other = pl.ds(pl.multiple_of((1 - d) * half, half), half)
    tile = 16
    for s in range(seqs):
        tok_copy(s).wait()

        def norm_rows(r, _):
            at = pl.ds(pl.multiple_of(r * tile, tile), tile)
            a = tok[s, at, mine].astype(jnp.float32)
            b = tok[s, at, other].astype(jnp.float32)
            total = jnp.sum(a * a, axis=-1, keepdims=True) + jnp.sum(b * b, axis=-1, keepdims=True)
            scale = lax.rsqrt(total * (1.0 / width) + EPS)
            lhs[s, at, :] = (a * scale * gain_ref[:, mine]).astype(jnp.bfloat16)
            xsend[s, at, :] = (b * scale * gain_ref[:, other]).astype(jnp.bfloat16)
            return 0

        lax.fori_loop(0, rows // tile, norm_rows, 0)
        if s == 0:
            pl.semaphore_wait(barrier, n)
        x_copy(s).start()

    def send_kb(t, _):
        kb_copy(peer(t), c).start()
        return 0

    lax.fori_loop(0, n - 1, send_kb, 0)
    pltpu.make_async_copy(kb_hbm, kb_all.at[c], kb_rsem.at[c]).start()

    def project(s, _):
        def step(t, _):
            @pl.when(t < n)
            def _():
                j = peer(t)
                u = s * n + t

                @pl.when(t == 0)
                def _():
                    x_copy(s).wait_recv()

                @pl.when(s == 0)
                def _():
                    for i in range(3):
                        w_copy(j, i).wait()

                acc = jnp.dot(lhs[s], wbuf[j], preferred_element_type=jnp.float32)
                psend[u] = acc[rows:]
                p_copy(u).start()
                pmine[t % (LAG + 1)] = acc[:rows]

            @pl.when(t >= LAG)
            def _():
                v = t - LAG
                j = peer(v)
                u = s * n + v
                p_copy(u).wait_recv()
                slot = v % (LAG + 1)
                for i, g_ref in enumerate((qg_ref, kg_ref)):
                    for h in range(heads):
                        at = pl.ds(i * cw + h * HEAD_DIM, HEAD_DIM)
                        raw = pmine[slot, :, at] + precv[u, :, at]
                        ms = jnp.mean(raw * raw, axis=-1, keepdims=True)
                        gains = g_ref[:, pl.ds(pl.multiple_of(j * cw + h * HEAD_DIM, HEAD_DIM), HEAD_DIM)]
                        send[s, j, :, at] = (raw * lax.rsqrt(ms + EPS) * gains).astype(jnp.bfloat16)
                at = pl.ds(2 * cw, cw)
                send[s, j, :, at] = (pmine[slot, :, at] + precv[u, :, at]).astype(jnp.bfloat16)

                @pl.when(v < n - 1)
                def _():
                    a_copy(s, j, c).start()

                @pl.when(v == n - 1)
                def _():
                    pltpu.make_async_copy(send.at[s, c], recvs[s].at[c], a_rsem.at[s, c]).start()

            return 0

        lax.fori_loop(0, n + LAG, step, 0)

    for s in range(seqs):
        project(s, 0)

    def wait_kb(j, _):
        kb_copy(j, j).wait_recv()
        return 0

    lax.fori_loop(0, n, wait_kb, 0)
    lists = pltpu.make_async_copy(kb_all, kb_smem, kb_lsem)
    lists.start()
    lists.wait()

    scale = 1.0 / float(HEAD_DIM) ** 0.5
    slots = 5
    for s in range(seqs):
        recv = recvs[s]

        def wait_block(j, _):
            a_copy(s, j, j).wait_recv()
            return 0

        lax.fori_loop(0, n, wait_block, 0)

        def attend(t, _):
            b = peer(t)
            listed = [kb_smem[b, 0, i] for i in range(slots)]
            for h in range(heads):
                lo = h * HEAD_DIM
                q = recv[b, :, pl.ds(lo, HEAD_DIM)]
                scores = []
                for kb in listed:
                    k = recv[kb, :, pl.ds(cw + lo, HEAD_DIM)]
                    scores.append(
                        lax.dot_general(q, k, (((1,), (1,)), ((), ())), preferred_element_type=jnp.float32) * scale
                    )
                top = functools.reduce(jnp.maximum, scores)
                row_max = jnp.max(top, axis=-1, keepdims=True)
                expo = [jnp.exp(x - row_max) for x in scores]
                total = jnp.sum(functools.reduce(jnp.add, expo), axis=-1, keepdims=True)
                mixed = None
                for e, kb in zip(expo, listed):
                    v = recv[kb, :, pl.ds(2 * cw + lo, HEAD_DIM)]
                    part = jnp.dot(e.astype(jnp.bfloat16), v, preferred_element_type=jnp.float32)
                    mixed = part if mixed is None else mixed + part
                obuf[s, b, :, pl.ds(lo, HEAD_DIM)] = (mixed / total).astype(jnp.bfloat16)

            @pl.when(t < n - 1)
            def _():
                o_copy(s, b, c).start()

            @pl.when(t == n - 1)
            def _():
                pltpu.make_async_copy(
                    obuf.at[s, c],
                    out_ref.at[s, :, pl.ds(pl.multiple_of(c * cw, cw), cw)],
                    o_rsem.at[s, c],
                ).start()

            return 0

        lax.fori_loop(0, n, attend, 0)

    def drain_p(u, _):
        p_copy(u).wait_send()
        return 0

    lax.fori_loop(0, steps, drain_p, 0)

    def drain_kb(t, _):
        kb_copy(peer(t), c).wait_send()
        return 0

    lax.fori_loop(0, n - 1, drain_kb, 0)
    for s in range(seqs):
        x_copy(s).wait_send()

        def drain(t, _):
            j = peer(t)
            a_copy(s, j, c).wait_send()
            o_copy(s, j, c).wait_send()
            return 0

        lax.fori_loop(0, n - 1, drain, 0)

        def arrive(j, _):
            o_copy(s, j, j).wait_recv()
            return 0

        lax.fori_loop(0, n, arrive, 0)


def shards(n, tokens, norm_gain, w_query, w_key, w_value, query_gain, key_gain, key_blocks):
    seqs, rows, width = tokens.shape
    half, hh = w_query.shape
    cw = hh // n
    bf, f32 = jnp.bfloat16, jnp.float32
    lists = jnp.pad(key_blocks, ((0, 7), (0, 128 - key_blocks.shape[1])))
    hbm = pl.BlockSpec(memory_space=pl.ANY)
    vmem = pl.BlockSpec(memory_space=pltpu.VMEM)
    dma = pltpu.SemaphoreType.DMA
    return pl.pallas_call(
        functools.partial(fused, n),
        out_shape=jax.ShapeDtypeStruct((seqs, rows, hh), bf),
        in_specs=[hbm, vmem, hbm, hbm, hbm, vmem, vmem, hbm],
        out_specs=hbm,
        scratch_shapes=[
            pltpu.VMEM((seqs, rows, width), bf),
            pltpu.VMEM((seqs, 2 * rows, half), bf),
            pltpu.VMEM((seqs, rows, half), bf),
            pltpu.VMEM((n, half, 3 * cw), bf),
            pltpu.VMEM((LAG + 1, rows, 3 * cw), f32),
            pltpu.VMEM((seqs * n, rows, 3 * cw), f32),
            pltpu.VMEM((seqs * n, rows, 3 * cw), f32),
            pltpu.VMEM((seqs, n, rows, 3 * cw), bf),
            pltpu.VMEM((n, rows, 3 * cw), bf),
            pltpu.VMEM((n, rows, 3 * cw), bf),
            pltpu.VMEM((seqs, n, rows, cw), bf),
            pltpu.VMEM((n, 8, 128), jnp.int32),
            pltpu.SMEM((n, 8, 128), jnp.int32),
            dma((seqs,)),
            dma((n, 3)),
            dma((seqs,)),
            dma((seqs,)),
            dma((seqs * n,)),
            dma((seqs * n,)),
            dma((seqs, n)),
            dma((seqs, n)),
            dma((seqs, n)),
            dma((seqs, n)),
            dma((n,)),
            dma((n,)),
            dma(()),
        ],
        compiler_params=pltpu.CompilerParams(
            collective_id=0, has_side_effects=True, vmem_limit_bytes=60 * 1024 * 1024
        ),
    )(
        tokens, norm_gain.reshape(1, width), w_query, w_key, w_value,
        query_gain.reshape(1, hh), key_gain.reshape(1, hh), lists,
    )


def solution(mesh):
    in_specs = (
        P(("groups", "dp"), "ctx", None),
        P(),
        P("dp", None),
        P("dp", None),
        P("dp", None),
        P(),
        P(),
        P(("groups", "ctx"), None),
    )
    out_specs = P(("groups", "dp"), "ctx", None)
    return jax.shard_map(
        functools.partial(shards, mesh.shape["ctx"]),
        mesh=mesh, in_specs=in_specs, out_specs=out_specs, check_vma=False,
    )
```

```python
import functools

import jax
import jax.numpy as jnp
from jax import lax
from jax.experimental import pallas as pl
from jax.experimental.pallas import tpu as pltpu
from jax.sharding import PartitionSpec as P

HEAD_DIM = 128
EPS = 1e-06
LAG = 2
MESH = pl.DeviceIdType.MESH


def fused(
    n,
    tok_hbm, gain_ref, wq_hbm, wk_hbm, wv_hbm, qg_ref, kg_ref, kb_hbm,
    out_ref,
    tok, lhs, xkeep, xsend, wbuf, pmine, psend, precv, send, recv_a, recv_b, obuf, kb_all, kb_smem,
    tok_sem, w_sem, x_ssem, x_rsem, p_ssem, p_rsem, a_ssem, a_rsem, o_ssem, o_rsem,
    kb_ssem, kb_rsem, kb_lsem, xf_ssem, xf_rsem,
):
    c = lax.axis_index("ctx")
    d = lax.axis_index("dp")
    seqs, rows, width = tok.shape
    half = width // 2
    cw = wbuf.shape[2] // 3
    heads = cw // HEAD_DIM
    recvs = (recv_a, recv_b)
    steps = seqs * n
    m = n // 2
    z = c // m
    across = (c + m) % n
    near = d == z
    far = d != z
    share = (c - z * m) * 2 + d
    block_a = (c + (d + z) % 2 * m) % n

    def peer(t):
        odd = t % 2
        off = n // 2 + (1 - odd) * (t // 2) - odd * ((t + 1) // 2)
        return (c + off) % n

    def peer_a(t):
        return ((c - z * m) * 2 + 2 + t) % n

    def chunk_at(s, t):
        return peer_a(t) if s == 0 else peer(t)

    def tok_copy(s):
        return pltpu.make_async_copy(tok_hbm.at[s], tok.at[s], tok_sem.at[s])

    def w_copy(j, i):
        w = (wq_hbm, wk_hbm, wv_hbm)[i]
        return pltpu.make_async_copy(
            w.at[:, pl.ds(pl.multiple_of(j * cw, cw), cw)],
            wbuf.at[j, :, pl.ds(i * cw, cw)],
            w_sem.at[j, i],
        )

    def x_copy(s):
        return pltpu.make_async_remote_copy(
            src_ref=xsend.at[s], dst_ref=lhs.at[s, pl.ds(rows, rows)],
            send_sem=x_ssem.at[s], recv_sem=x_rsem.at[s],
            device_id={"dp": 1 - d}, device_id_type=MESH)

    def p_copy(u):
        return pltpu.make_async_remote_copy(
            src_ref=psend.at[u], dst_ref=precv.at[u],
            send_sem=p_ssem.at[u], recv_sem=p_rsem.at[u],
            device_id={"dp": 1 - d}, device_id_type=MESH)

    def xf_copy(src_ref, at, send_sem, recv_sem, core):
        return pltpu.make_async_remote_copy(
            src_ref=src_ref, dst_ref=lhs.at[0, pl.ds(at, rows)],
            send_sem=send_sem, recv_sem=recv_sem,
            device_id={"ctx": across, "dp": core}, device_id_type=MESH)

    def xf_keep():
        return xf_copy(xkeep, rows, xf_ssem, x_rsem.at[0], d)

    def xf_send():
        return xf_copy(xsend.at[0], 0, x_ssem.at[0], xf_rsem, 1 - d)

    def a_copy(s, j, src):
        if s == 0:
            return pltpu.make_async_remote_copy(
                src_ref=send.at[0, j], dst_ref=recv_a.at[src],
                send_sem=a_ssem.at[0, j], recv_sem=a_rsem.at[0, src],
                device_id={"ctx": z * m + j // 2, "dp": j % 2}, device_id_type=MESH)
        return pltpu.make_async_remote_copy(
            src_ref=send.at[s, j], dst_ref=recvs[s].at[src],
            send_sem=a_ssem.at[s, j], recv_sem=a_rsem.at[s, src],
            device_id={"ctx": j}, device_id_type=MESH)

    def o_copy(s, j, src):
        return pltpu.make_async_remote_copy(
            src_ref=obuf.at[s, j],
            dst_ref=out_ref.at[s, :, pl.ds(pl.multiple_of(src * cw, cw), cw)],
            send_sem=o_ssem.at[s, j], recv_sem=o_rsem.at[s, src],
            device_id={"ctx": j, "dp": z} if s == 0 else {"ctx": j}, device_id_type=MESH)

    def kb_copy(j, src):
        return pltpu.make_async_remote_copy(
            src_ref=kb_hbm, dst_ref=kb_all.at[src],
            send_sem=kb_ssem.at[j], recv_sem=kb_rsem.at[src],
            device_id={"ctx": j}, device_id_type=MESH)

    for s in range(seqs):
        tok_copy(s).start()

    def start_weights(t, _):
        for i in range(3):
            w_copy(peer(t), i).start()
        return 0

    lax.fori_loop(0, n, start_weights, 0)

    barrier = pltpu.get_barrier_semaphore()

    def greet_other(t, _):
        pl.semaphore_signal(
            barrier, inc=1, device_id={"ctx": peer(t), "dp": 1 - d}, device_id_type=MESH)
        return 0

    lax.fori_loop(0, n, greet_other, 0)

    def greet(t, _):
        pl.semaphore_signal(barrier, inc=1, device_id={"ctx": peer(t)}, device_id_type=MESH)
        return 0

    lax.fori_loop(0, n - 1, greet, 0)

    mine = pl.ds(pl.multiple_of(d * half, half), half)
    other = pl.ds(pl.multiple_of((1 - d) * half, half), half)
    tile = 16
    for s in range(seqs):
        tok_copy(s).wait()

        def norm_rows(r, _):
            at = pl.ds(pl.multiple_of(r * tile, tile), tile)
            a = tok[s, at, mine].astype(jnp.float32)
            b = tok[s, at, other].astype(jnp.float32)
            total = jnp.sum(a * a, axis=-1, keepdims=True) + jnp.sum(b * b, axis=-1, keepdims=True)
            scale = lax.rsqrt(total * (1.0 / width) + EPS)
            held = xkeep if s == 0 else lhs.at[s]
            held[at, :] = (a * scale * gain_ref[:, mine]).astype(jnp.bfloat16)
            xsend[s, at, :] = (b * scale * gain_ref[:, other]).astype(jnp.bfloat16)
            return 0

        lax.fori_loop(0, rows // tile, norm_rows, 0)
        if s == 0:
            pl.semaphore_wait(barrier, 2 * n - 1)

            @pl.when(far)
            def _():
                xf_send().start()
                xf_keep().start()

            @pl.when(near)
            def _():
                x_copy(0).start()
                pltpu.make_async_copy(xkeep, lhs.at[0, pl.ds(0, rows)], xf_rsem).start()
        else:
            x_copy(s).start()

    def send_kb(t, _):
        kb_copy(peer(t), c).start()
        return 0

    lax.fori_loop(0, n - 1, send_kb, 0)
    pltpu.make_async_copy(kb_hbm, kb_all.at[c], kb_rsem.at[c]).start()

    def project(s, _):
        def step(t, _):
            @pl.when(t < n)
            def _():
                j = chunk_at(s, t)
                u = s * n + t

                @pl.when(t == 0)
                def _():
                    x_copy(s).wait_recv()
                    if s == 0:
                        xf_send().wait_recv()

                if s == seqs - 1:
                    for i in range(3):
                        w_copy(j, i).wait()

                acc = jnp.dot(lhs[s], wbuf[j], preferred_element_type=jnp.float32)
                psend[u] = acc[rows:]
                p_copy(u).start()
                pmine[t % (LAG + 1)] = acc[:rows]

            @pl.when(t >= LAG)
            def _():
                v = t - LAG
                j = chunk_at(s, v)
                u = s * n + v
                p_copy(u).wait_recv()
                slot = v % (LAG + 1)
                for i, g_ref in enumerate((qg_ref, kg_ref)):
                    for h in range(heads):
                        at = pl.ds(i * cw + h * HEAD_DIM, HEAD_DIM)
                        raw = pmine[slot, :, at] + precv[u, :, at]
                        ms = jnp.mean(raw * raw, axis=-1, keepdims=True)
                        gains = g_ref[:, pl.ds(pl.multiple_of(j * cw + h * HEAD_DIM, HEAD_DIM), HEAD_DIM)]
                        send[s, j, :, at] = (raw * lax.rsqrt(ms + EPS) * gains).astype(jnp.bfloat16)
                at = pl.ds(2 * cw, cw)
                send[s, j, :, at] = (pmine[slot, :, at] + precv[u, :, at]).astype(jnp.bfloat16)

                leaves = j != share if s == 0 else v < n - 1

                @pl.when(leaves)
                def _():
                    a_copy(s, j, block_a if s == 0 else c).start()

                @pl.when(jnp.logical_not(leaves))
                def _():
                    own = block_a if s == 0 else c
                    pltpu.make_async_copy(send.at[s, j], recvs[s].at[own], a_rsem.at[s, own]).start()

            return 0

        lax.fori_loop(0, n + LAG, step, 0)

    for s in reversed(range(seqs)):
        project(s, 0)

    def wait_kb(j, _):
        kb_copy(j, j).wait_recv()
        return 0

    lax.fori_loop(0, n, wait_kb, 0)
    lists = pltpu.make_async_copy(kb_all, kb_smem, kb_lsem)
    lists.start()
    lists.wait()

    scale = 1.0 / float(HEAD_DIM) ** 0.5
    slots = 5
    for s in reversed(range(seqs)):
        recv = recvs[s]
        part = share if s == 0 else c

        def wait_block(j, _):
            a_copy(s, j, j).wait_recv()
            return 0

        lax.fori_loop(0, n, wait_block, 0)

        def attend(t, _):
            b = peer(t)
            listed = [kb_smem[b, 0, i] for i in range(slots)]
            for h in range(heads):
                lo = h * HEAD_DIM
                q = recv[b, :, pl.ds(lo, HEAD_DIM)]
                scores = []
                for kb in listed:
                    k = recv[kb, :, pl.ds(cw + lo, HEAD_DIM)]
                    scores.append(
                        lax.dot_general(q, k, (((1,), (1,)), ((), ())), preferred_element_type=jnp.float32) * scale
                    )
                top = functools.reduce(jnp.maximum, scores)
                row_max = jnp.max(top, axis=-1, keepdims=True)
                expo = [jnp.exp(x - row_max) for x in scores]
                total = jnp.sum(functools.reduce(jnp.add, expo), axis=-1, keepdims=True)
                mixed = None
                for e, kb in zip(expo, listed):
                    v = recv[kb, :, pl.ds(2 * cw + lo, HEAD_DIM)]
                    piece = jnp.dot(e.astype(jnp.bfloat16), v, preferred_element_type=jnp.float32)
                    mixed = piece if mixed is None else mixed + piece
                obuf[s, b, :, pl.ds(lo, HEAD_DIM)] = (mixed / total).astype(jnp.bfloat16)

            remote = (t < n - 1) | far if s == 0 else t < n - 1

            @pl.when(remote)
            def _():
                o_copy(s, b, part).start()

            @pl.when(jnp.logical_not(remote))
            def _():
                pltpu.make_async_copy(
                    obuf.at[s, c],
                    out_ref.at[s, :, pl.ds(pl.multiple_of(part * cw, cw), cw)],
                    o_rsem.at[s, part],
                ).start()

            return 0

        lax.fori_loop(0, n, attend, 0)

    def drain_p(u, _):
        p_copy(u).wait_send()
        return 0

    lax.fori_loop(0, steps, drain_p, 0)

    def drain_kb(t, _):
        kb_copy(peer(t), c).wait_send()
        return 0

    lax.fori_loop(0, n - 1, drain_kb, 0)

    @pl.when(far)
    def _():
        xf_keep().wait_send()
        o_copy(0, c, share).wait_send()

    for s in range(seqs):
        x_copy(s).wait_send()

        def drain(t, _):
            a_copy(s, (share + 1 + t) % n if s == 0 else peer(t), c).wait_send()
            o_copy(s, peer(t), c).wait_send()
            return 0

        lax.fori_loop(0, n - 1, drain, 0)

        def arrive(j, _):
            o_copy(s, j, j).wait_recv()
            return 0

        lax.fori_loop(0, n, arrive, 0)


def shards(n, tokens, norm_gain, w_query, w_key, w_value, query_gain, key_gain, key_blocks):
    seqs, rows, width = tokens.shape
    half, hh = w_query.shape
    cw = hh // n
    bf, f32 = jnp.bfloat16, jnp.float32
    lists = jnp.pad(key_blocks, ((0, 7), (0, 128 - key_blocks.shape[1])))
    hbm = pl.BlockSpec(memory_space=pl.ANY)
    vmem = pl.BlockSpec(memory_space=pltpu.VMEM)
    dma = pltpu.SemaphoreType.DMA
    return pl.pallas_call(
        functools.partial(fused, n),
        out_shape=jax.ShapeDtypeStruct((seqs, rows, hh), bf),
        in_specs=[hbm, vmem, hbm, hbm, hbm, vmem, vmem, hbm],
        out_specs=hbm,
        scratch_shapes=[
            pltpu.VMEM((seqs, rows, width), bf),
            pltpu.VMEM((seqs, 2 * rows, half), bf),
            pltpu.VMEM((rows, half), bf),
            pltpu.VMEM((seqs, rows, half), bf),
            pltpu.VMEM((n, half, 3 * cw), bf),
            pltpu.VMEM((LAG + 1, rows, 3 * cw), f32),
            pltpu.VMEM((seqs * n, rows, 3 * cw), f32),
            pltpu.VMEM((seqs * n, rows, 3 * cw), f32),
            pltpu.VMEM((seqs, n, rows, 3 * cw), bf),
            pltpu.VMEM((n, rows, 3 * cw), bf),
            pltpu.VMEM((n, rows, 3 * cw), bf),
            pltpu.VMEM((seqs, n, rows, cw), bf),
            pltpu.VMEM((n, 8, 128), jnp.int32),
            pltpu.SMEM((n, 8, 128), jnp.int32),
            dma((seqs,)),
            dma((n, 3)),
            dma((seqs,)),
            dma((seqs,)),
            dma((seqs * n,)),
            dma((seqs * n,)),
            dma((seqs, n)),
            dma((seqs, n)),
            dma((seqs, n)),
            dma((seqs, n)),
            dma((n,)),
            dma((n,)),
            dma(()),
            dma(()),
            dma(()),
        ],
        compiler_params=pltpu.CompilerParams(
            collective_id=0, has_side_effects=True, vmem_limit_bytes=60 * 1024 * 1024
        ),
    )(
        tokens, norm_gain.reshape(1, width), w_query, w_key, w_value,
        query_gain.reshape(1, hh), key_gain.reshape(1, hh), lists,
    )


def solution(mesh):
    in_specs = (
        P(("groups", "dp"), "ctx", None),
        P(),
        P("dp", None),
        P("dp", None),
        P("dp", None),
        P(),
        P(),
        P(("groups", "ctx"), None),
    )
    out_specs = P(("groups", "dp"), "ctx", None)
    return jax.shard_map(
        functools.partial(shards, mesh.shape["ctx"]),
        mesh=mesh, in_specs=in_specs, out_specs=out_specs, check_vma=False,
    )
```

```python
import functools

import jax
import jax.numpy as jnp
from jax import lax
from jax.experimental import pallas as pl
from jax.experimental.pallas import tpu as pltpu
from jax.sharding import PartitionSpec as P

HEAD_DIM = 128
EPS = 1e-06
LAG = 2
MESH = pl.DeviceIdType.MESH


def fused(
    n,
    tok_hbm, gain_ref, wq_hbm, wk_hbm, wv_hbm, qg_ref, kg_ref, kb_hbm,
    out_ref,
    tok, lhs, xkeep, xsend, wbuf, pmine, psend, precv, send, recv_a, recv_b, obuf, kb_all, kb_smem,
    tok_sem, w_sem, x_ssem, x_rsem, p_ssem, p_rsem, a_ssem, a_rsem, o_ssem, o_rsem,
    kb_ssem, kb_rsem, kb_lsem, xf_ssem, xf_rsem,
):
    c = lax.axis_index("ctx")
    d = lax.axis_index("dp")
    seqs, rows, width = tok.shape
    half = width // 2
    cw = wbuf.shape[2] // 3
    heads = cw // HEAD_DIM
    recvs = (recv_a, recv_b)
    steps = seqs * n
    m = n // 2
    z = c // m
    across = (c + m) % n
    near = d == z
    far = d != z
    share = (c - z * m) * 2 + d
    block_a = (c + (d + z) % 2 * m) % n

    def peer(t):
        odd = t % 2
        off = n // 2 + (1 - odd) * (t // 2) - odd * ((t + 1) // 2)
        return (c + off) % n

    def peer_a(t):
        return ((c - z * m) * 2 + 2 + t) % n

    def chunk_at(s, t):
        return peer_a(t) if s == 0 else peer(t)

    def tok_copy(s):
        return pltpu.make_async_copy(tok_hbm.at[s], tok.at[s], tok_sem.at[s])

    def w_copy(j, i):
        w = (wq_hbm, wk_hbm, wv_hbm)[i]
        return pltpu.make_async_copy(
            w.at[:, pl.ds(pl.multiple_of(j * cw, cw), cw)],
            wbuf.at[j, :, pl.ds(i * cw, cw)],
            w_sem.at[j, i],
        )

    def x_copy(s):
        return pltpu.make_async_remote_copy(
            src_ref=xsend.at[s], dst_ref=lhs.at[s, pl.ds(rows, rows)],
            send_sem=x_ssem.at[s], recv_sem=x_rsem.at[s],
            device_id={"dp": 1 - d}, device_id_type=MESH)

    def p_copy(u):
        return pltpu.make_async_remote_copy(
            src_ref=psend.at[u], dst_ref=precv.at[u],
            send_sem=p_ssem.at[u], recv_sem=p_rsem.at[u],
            device_id={"dp": 1 - d}, device_id_type=MESH)

    def xf_copy(src_ref, at, send_sem, recv_sem, core):
        return pltpu.make_async_remote_copy(
            src_ref=src_ref, dst_ref=lhs.at[0, pl.ds(at, rows)],
            send_sem=send_sem, recv_sem=recv_sem,
            device_id={"ctx": across, "dp": core}, device_id_type=MESH)

    def xf_keep():
        return xf_copy(xkeep, rows, xf_ssem, x_rsem.at[0], d)

    def xf_send():
        return xf_copy(xsend.at[0], 0, x_ssem.at[0], xf_rsem, 1 - d)

    def a_copy(s, j, src):
        if s == 0:
            return pltpu.make_async_remote_copy(
                src_ref=send.at[0, j], dst_ref=recv_a.at[src],
                send_sem=a_ssem.at[0, j], recv_sem=a_rsem.at[0, src],
                device_id={"ctx": z * m + j // 2, "dp": j % 2}, device_id_type=MESH)
        return pltpu.make_async_remote_copy(
            src_ref=send.at[s, j], dst_ref=recvs[s].at[src],
            send_sem=a_ssem.at[s, j], recv_sem=a_rsem.at[s, src],
            device_id={"ctx": j}, device_id_type=MESH)

    def o_copy(s, j, src):
        return pltpu.make_async_remote_copy(
            src_ref=obuf.at[s, j],
            dst_ref=out_ref.at[s, :, pl.ds(pl.multiple_of(src * cw, cw), cw)],
            send_sem=o_ssem.at[s, j], recv_sem=o_rsem.at[s, src],
            device_id={"ctx": j, "dp": z} if s == 0 else {"ctx": j}, device_id_type=MESH)

    def kb_copy(j, src):
        return pltpu.make_async_remote_copy(
            src_ref=kb_hbm, dst_ref=kb_all.at[src],
            send_sem=kb_ssem.at[j], recv_sem=kb_rsem.at[src],
            device_id={"ctx": j}, device_id_type=MESH)

    for s in range(seqs):
        tok_copy(s).start()

    def start_weights(t, _):
        for i in range(3):
            w_copy(peer(t), i).start()
        return 0

    lax.fori_loop(0, n, start_weights, 0)

    barrier = pltpu.get_barrier_semaphore()

    def greet_other(t, _):
        pl.semaphore_signal(
            barrier, inc=1, device_id={"ctx": peer(t), "dp": 1 - d}, device_id_type=MESH)
        return 0

    lax.fori_loop(0, n, greet_other, 0)

    def greet(t, _):
        pl.semaphore_signal(barrier, inc=1, device_id={"ctx": peer(t)}, device_id_type=MESH)
        return 0

    lax.fori_loop(0, n - 1, greet, 0)

    mine = pl.ds(pl.multiple_of(d * half, half), half)
    other = pl.ds(pl.multiple_of((1 - d) * half, half), half)
    tile = 16
    for s in range(seqs):
        tok_copy(s).wait()

        def norm_rows(r, _):
            at = pl.ds(pl.multiple_of(r * tile, tile), tile)
            a = tok[s, at, mine].astype(jnp.float32)
            b = tok[s, at, other].astype(jnp.float32)
            total = jnp.sum(a * a, axis=-1, keepdims=True) + jnp.sum(b * b, axis=-1, keepdims=True)
            scale = lax.rsqrt(total * (1.0 / width) + EPS)
            held = xkeep if s == 0 else lhs.at[s]
            held[at, :] = (a * scale * gain_ref[:, mine]).astype(jnp.bfloat16)
            xsend[s, at, :] = (b * scale * gain_ref[:, other]).astype(jnp.bfloat16)
            return 0

        lax.fori_loop(0, rows // tile, norm_rows, 0)
        if s == 0:
            pl.semaphore_wait(barrier, 2 * n - 1)

            @pl.when(far)
            def _():
                xf_send().start()
                xf_keep().start()

            @pl.when(near)
            def _():
                x_copy(0).start()
                pltpu.make_async_copy(xkeep, lhs.at[0, pl.ds(0, rows)], xf_rsem).start()
        else:
            x_copy(s).start()

    def send_kb(t, _):
        kb_copy(peer(t), c).start()
        return 0

    lax.fori_loop(0, n - 1, send_kb, 0)
    pltpu.make_async_copy(kb_hbm, kb_all.at[c], kb_rsem.at[c]).start()

    def send_across(t, _):
        j = peer(t)

        @pl.when(j // m != z)
        def _():
            a_copy(seqs - 1, j, c).start()

        return 0

    def project(s, _):
        def step(t, _):
            @pl.when(t < n)
            def _():
                j = chunk_at(s, t)
                u = s * n + t

                @pl.when(t == 0)
                def _():
                    x_copy(s).wait_recv()
                    if s == 0:
                        xf_send().wait_recv()
                        lax.fori_loop(0, n - 1, send_across, 0)

                if s == seqs - 1:
                    for i in range(3):
                        w_copy(j, i).wait()

                acc = jnp.dot(lhs[s], wbuf[j], preferred_element_type=jnp.float32)
                psend[u] = acc[rows:]
                p_copy(u).start()
                pmine[t % (LAG + 1)] = acc[:rows]

            @pl.when(t >= LAG)
            def _():
                v = t - LAG
                j = chunk_at(s, v)
                u = s * n + v
                p_copy(u).wait_recv()
                slot = v % (LAG + 1)
                for i, g_ref in enumerate((qg_ref, kg_ref)):
                    for h in range(heads):
                        at = pl.ds(i * cw + h * HEAD_DIM, HEAD_DIM)
                        raw = pmine[slot, :, at] + precv[u, :, at]
                        ms = jnp.mean(raw * raw, axis=-1, keepdims=True)
                        gains = g_ref[:, pl.ds(pl.multiple_of(j * cw + h * HEAD_DIM, HEAD_DIM), HEAD_DIM)]
                        send[s, j, :, at] = (raw * lax.rsqrt(ms + EPS) * gains).astype(jnp.bfloat16)
                at = pl.ds(2 * cw, cw)
                send[s, j, :, at] = (pmine[slot, :, at] + precv[u, :, at]).astype(jnp.bfloat16)

                leaves = j != share if s == 0 else v < n - 1
                early = leaves if s == 0 else leaves & (j // m == z)

                @pl.when(early)
                def _():
                    a_copy(s, j, block_a if s == 0 else c).start()

                @pl.when(jnp.logical_not(leaves))
                def _():
                    own = block_a if s == 0 else c
                    pltpu.make_async_copy(send.at[s, j], recvs[s].at[own], a_rsem.at[s, own]).start()

            return 0

        lax.fori_loop(0, n + LAG, step, 0)

    for s in reversed(range(seqs)):
        project(s, 0)

    def wait_kb(j, _):
        kb_copy(j, j).wait_recv()
        return 0

    lax.fori_loop(0, n, wait_kb, 0)
    lists = pltpu.make_async_copy(kb_all, kb_smem, kb_lsem)
    lists.start()
    lists.wait()

    scale = 1.0 / float(HEAD_DIM) ** 0.5
    slots = 5
    for s in reversed(range(seqs)):
        recv = recvs[s]
        part = share if s == 0 else c

        def wait_block(j, _):
            a_copy(s, j, j).wait_recv()
            return 0

        lax.fori_loop(0, n, wait_block, 0)

        def attend(t, _):
            b = peer(t)
            listed = [kb_smem[b, 0, i] for i in range(slots)]
            for h in range(heads):
                lo = h * HEAD_DIM
                q = recv[b, :, pl.ds(lo, HEAD_DIM)]
                scores = []
                for kb in listed:
                    k = recv[kb, :, pl.ds(cw + lo, HEAD_DIM)]
                    scores.append(
                        lax.dot_general(q, k, (((1,), (1,)), ((), ())), preferred_element_type=jnp.float32) * scale
                    )
                top = functools.reduce(jnp.maximum, scores)
                row_max = jnp.max(top, axis=-1, keepdims=True)
                expo = [jnp.exp(x - row_max) for x in scores]
                total = jnp.sum(functools.reduce(jnp.add, expo), axis=-1, keepdims=True)
                mixed = None
                for e, kb in zip(expo, listed):
                    v = recv[kb, :, pl.ds(2 * cw + lo, HEAD_DIM)]
                    piece = jnp.dot(e.astype(jnp.bfloat16), v, preferred_element_type=jnp.float32)
                    mixed = piece if mixed is None else mixed + piece
                obuf[s, b, :, pl.ds(lo, HEAD_DIM)] = (mixed / total).astype(jnp.bfloat16)

            remote = (t < n - 1) | far if s == 0 else t < n - 1

            @pl.when(remote)
            def _():
                o_copy(s, b, part).start()

            @pl.when(jnp.logical_not(remote))
            def _():
                pltpu.make_async_copy(
                    obuf.at[s, c],
                    out_ref.at[s, :, pl.ds(pl.multiple_of(part * cw, cw), cw)],
                    o_rsem.at[s, part],
                ).start()

            return 0

        lax.fori_loop(0, n, attend, 0)

    def drain_p(u, _):
        p_copy(u).wait_send()
        return 0

    lax.fori_loop(0, steps, drain_p, 0)

    def drain_kb(t, _):
        kb_copy(peer(t), c).wait_send()
        return 0

    lax.fori_loop(0, n - 1, drain_kb, 0)

    @pl.when(far)
    def _():
        xf_keep().wait_send()
        o_copy(0, c, share).wait_send()

    for s in range(seqs):
        x_copy(s).wait_send()

        def drain(t, _):
            a_copy(s, (share + 1 + t) % n if s == 0 else peer(t), c).wait_send()
            o_copy(s, peer(t), c).wait_send()
            return 0

        lax.fori_loop(0, n - 1, drain, 0)

        def arrive(j, _):
            o_copy(s, j, j).wait_recv()
            return 0

        lax.fori_loop(0, n, arrive, 0)


def shards(n, tokens, norm_gain, w_query, w_key, w_value, query_gain, key_gain, key_blocks):
    seqs, rows, width = tokens.shape
    half, hh = w_query.shape
    cw = hh // n
    bf, f32 = jnp.bfloat16, jnp.float32
    hbm = pl.BlockSpec(memory_space=pl.ANY)
    vmem = pl.BlockSpec(memory_space=pltpu.VMEM)
    dma = pltpu.SemaphoreType.DMA
    return pl.pallas_call(
        functools.partial(fused, n),
        out_shape=jax.ShapeDtypeStruct((seqs, rows, hh), bf),
        in_specs=[hbm, vmem, hbm, hbm, hbm, vmem, vmem, hbm],
        out_specs=hbm,
        scratch_shapes=[
            pltpu.VMEM((seqs, rows, width), bf),
            pltpu.VMEM((seqs, 2 * rows, half), bf),
            pltpu.VMEM((rows, half), bf),
            pltpu.VMEM((seqs, rows, half), bf),
            pltpu.VMEM((n, half, 3 * cw), bf),
            pltpu.VMEM((LAG + 1, rows, 3 * cw), f32),
            pltpu.VMEM((seqs * n, rows, 3 * cw), f32),
            pltpu.VMEM((seqs * n, rows, 3 * cw), f32),
            pltpu.VMEM((seqs, n, rows, 3 * cw), bf),
            pltpu.VMEM((n, rows, 3 * cw), bf),
            pltpu.VMEM((n, rows, 3 * cw), bf),
            pltpu.VMEM((seqs, n, rows, cw), bf),
            pltpu.VMEM((n,) + key_blocks.shape, jnp.int32),
            pltpu.SMEM((n,) + key_blocks.shape, jnp.int32),
            dma((seqs,)),
            dma((n, 3)),
            dma((seqs,)),
            dma((seqs,)),
            dma((seqs * n,)),
            dma((seqs * n,)),
            dma((seqs, n)),
            dma((seqs, n)),
            dma((seqs, n)),
            dma((seqs, n)),
            dma((n,)),
            dma((n,)),
            dma(()),
            dma(()),
            dma(()),
        ],
        compiler_params=pltpu.CompilerParams(
            collective_id=0, has_side_effects=True, vmem_limit_bytes=60 * 1024 * 1024
        ),
    )(
        tokens, norm_gain.reshape(1, width), w_query, w_key, w_value,
        query_gain.reshape(1, hh), key_gain.reshape(1, hh), key_blocks,
    )


def solution(mesh):
    in_specs = (
        P(("groups", "dp"), "ctx", None),
        P(),
        P("dp", None),
        P("dp", None),
        P("dp", None),
        P(),
        P(),
        P(("groups", "ctx"), None),
    )
    out_specs = P(("groups", "dp"), "ctx", None)
    return jax.shard_map(
        functools.partial(shards, mesh.shape["ctx"]),
        mesh=mesh, in_specs=in_specs, out_specs=out_specs, check_vma=False,
    )
```
